256 devices in a mesh: group: 32 (over z, x), tensor: 8 (over y, core).
Axes of the slice: x: 4, y: 4, z: 8, core: 2. Of those that a mesh axis runs over, the one named last changes fastest.
Arguments:
- hidden: bfloat16 [8192, 7168], P('group', 'tensor'), may hold values from -6 to 6
- w_kv_a: bfloat16 [7168, 576], P('tensor'), may hold values from -0.0625 to 0.0625
- kv_gain: float32 [512], replicated, may hold values from 0.5 to 1.5
- q_latent: bfloat16 [8192, 1536], P('group'), may hold values from -6 to 6
- w_q_b: bfloat16 [1536, 12288], P(None, 'tensor'), may hold values from -0.15625 to 0.15625
- w_key_up: bfloat16 [512, 8192], P(None, 'tensor'), may hold values from -0.5 to 0.5
- w_value_up: bfloat16 [512, 8192], P(None, 'tensor'), may hold values from -0.25 to 0.25
- pool: bfloat16 [4096, 32, 576], P('group', 'tensor'), may hold values from -170 to 170
- page_table: int32 [32, 64], replicated, may hold values from 0 to 4095, as said below
- prefix_len: int32 [32], replicated, may hold values from 32 to 2048, as said below
- decode_owner: int32 [32], replicated, may hold values from 0 to 31, each once
Outputs:
- attn_out: bfloat16 [8192, 8192], P('group', 'tensor')
- decode_pages: bfloat16 [8192, 576], P(('group', 'tensor'))
The draws below stay inside these ranges and needn't reach their ends.
Inputs may be any that keep to these rules, and one draw needn't show every extreme that they name: `page_table`: each row names every owner group (page id // 128) exactly 2 times; no page id appears twice in the whole table. `prefix_len`: the largest value is reached in every draw. `decode_owner`: a permutation of the groups.
All inputs are finite; a program needn't handle non-finite values.
Results may differ from the reference program's by a relative error of at most 0.012.
Values may be sent and summed in bfloat16 or wider, within the bound.
No kernel may reach another device: no remote copies, remote signals or barrier semaphores. Data moves between devices by JAX's collectives and lax.ppermute only.
A program may use at most 128 MiB of HBM per device.

```python
import jax
import jax.numpy as jnp
from jax import lax

D = 7168
H = 64
NOPE = 128
ROPE = 64
VDIM = 128
KVR = 512
QR = 1536
NEW = 256
PAGE = 32
CAP = 2
SLOTS = 128
LAT = 576
MAXP = 64
N_GROUP = 32


def draw_pool(key, part):
    key = jax.random.fold_in(key, 31)
    base_key = jax.random.fold_in(key, 0)
    pages = N_GROUP * SLOTS
    values = jnp.clip(jax.random.normal(base_key, (pages, PAGE, LAT), jnp.float32), -6.0, 6.0)
    return values.astype(jnp.bfloat16)


def draw_page_table(key, part):
    key = jax.random.fold_in(key, 11)
    order_key, slot_key = jax.random.split(key)
    orders = jax.vmap(lambda subkey: jax.random.permutation(subkey, CAP * N_GROUP))(jax.random.split(order_key, N_GROUP))
    owners = orders // CAP
    within = orders % CAP
    slot_orders = jax.vmap(lambda subkey: jax.random.permutation(subkey, SLOTS))(jax.random.split(slot_key, N_GROUP))
    requests = jnp.arange(N_GROUP, dtype=jnp.int32)[:, None]
    slots = slot_orders[owners, requests * CAP + within]
    return (owners * SLOTS + slots).astype(jnp.int32)


def draw_prefix_len(key, part):
    key = jax.random.fold_in(key, 23)
    first_key, second_key, pick_key = jax.random.split(key, 3)
    longest = CAP * N_GROUP * PAGE
    first = jax.random.randint(first_key, (N_GROUP,), PAGE, longest + 1)
    second = jax.random.randint(second_key, (N_GROUP,), PAGE, longest + 1)
    lengths = jnp.minimum(first, second)
    chosen = jax.random.randint(pick_key, (), 0, N_GROUP)
    lengths = jnp.where(jnp.arange(N_GROUP) == chosen, longest, lengths)
    return lengths.astype(jnp.int32)


def steps_of(own_key, shape, cuts, low, high):
    level = 1.0
    for position, parts in cuts:
        draws = jax.random.uniform(jax.random.fold_in(jax.random.fold_in(own_key, 6), position), (parts,), jnp.float32, low / len(cuts), high / len(cuts))
        level = level * jnp.repeat(jnp.exp(draws), shape[position] // parts).reshape((-1,) + (1,) * (len(shape) - 1 - position))
    return level


def bell_draw(stream_key, extent, scale, limit, pieces=(), kind=jnp.bfloat16):
    result = scale * jax.random.normal(stream_key, extent, jnp.float32)
    if pieces:
        result = result * steps_of(stream_key, extent, pieces, -0.22, 0.18)
    return jnp.clip(result, -limit, limit).astype(kind)


def setup_inputs(seed: int = 0) -> dict:
    key_of = jax.random.split(jax.random.key(seed), 12)
    return {
        "hidden": bell_draw(key_of[0], (N_GROUP * NEW, D), 1.0, 6.0, ((0, 32), (1, 8))),
        "w_kv_a": bell_draw(key_of[1], (D, LAT), D ** -0.5, 0.0625, ((0, 8),)),
        "kv_gain": jnp.clip(1.0 + 0.1 * jax.random.normal(key_of[2], (KVR,), jnp.float32), 0.5, 1.5),
        "q_latent": bell_draw(key_of[3], (N_GROUP * NEW, QR), 1.0, 6.0, ((0, 32),)),
        "w_q_b": bell_draw(key_of[4], (QR, H * (NOPE + ROPE)), QR ** -0.5, 0.15625, ((1, 8),)),
        "w_key_up": bell_draw(key_of[5], (KVR, H * NOPE), NOPE ** -0.5, 0.5, ((1, 8),)),
        "w_value_up": bell_draw(key_of[6], (KVR, H * VDIM), KVR ** -0.5, 0.25, ((1, 8),)),
        "pool": draw_pool(jax.random.fold_in(key_of[11], 71), 0),
        "page_table": draw_page_table(jax.random.fold_in(key_of[11], 71), 0),
        "prefix_len": draw_prefix_len(jax.random.fold_in(key_of[11], 71), 0),
        "decode_owner": jax.random.permutation(key_of[10], N_GROUP).astype(jnp.int32),
    }


rope_base = 50000.0
masked_value = -1e+30

def apply_rope(values, positions):
    half_width = values.shape[-1] // 2
    frequency = rope_base ** (-2.0 * jnp.arange(half_width, dtype=jnp.float32) / values.shape[-1])
    angles = positions.astype(jnp.float32)[:, None] * frequency[None, :]
    angles = angles.reshape(angles.shape[:1] + (1,) * (values.ndim - 2) + angles.shape[1:])
    cosine = jnp.cos(angles)
    sine = jnp.sin(angles)
    first = values[..., :half_width]
    second = values[..., half_width:]
    return jnp.concatenate([first * cosine - second * sine, second * cosine + first * sine], axis=-1)

def finish_latent(projected, positions, kv_gain):
    nope_part = projected[:, :KVR]
    mean_square = lax.optimization_barrier(jnp.mean(nope_part * nope_part, axis=-1, keepdims=True))
    normed = nope_part * lax.rsqrt(mean_square + 1e-06) * kv_gain
    rotated = apply_rope(projected[:, KVR:], positions)
    return jnp.concatenate([normed, rotated], axis=-1).astype(jnp.bfloat16)

def reference(hidden, w_kv_a, kv_gain, q_latent, w_q_b, w_key_up, w_value_up, pool, page_table, prefix_len, decode_owner):
    scale = float(NOPE + ROPE) ** (-0.5)
    prefix_tokens = MAXP * PAGE
    key_up = w_key_up.reshape(KVR, H, NOPE).astype(jnp.float32)
    value_up = w_value_up.reshape(KVR, H, VDIM).astype(jnp.float32)

    def one_request(inputs):
        hidden_rows, query_latent, table_row, length = inputs
        positions = length + jnp.arange(NEW, dtype=jnp.int32)
        latent = finish_latent(jnp.dot(hidden_rows, w_kv_a, preferred_element_type=jnp.float32), positions, kv_gain)
        q_full = jnp.dot(query_latent, w_q_b, preferred_element_type=jnp.float32).reshape(NEW, H, NOPE + ROPE)
        q_nope = q_full[..., :NOPE].astype(jnp.bfloat16)
        q_rope = apply_rope(q_full[..., NOPE:], positions).astype(jnp.bfloat16)
        absorbed = jnp.einsum('nhd,chd->nhc', q_nope.astype(jnp.float32), key_up).astype(jnp.bfloat16)
        query_rows = jnp.concatenate([absorbed, q_rope], axis=-1)
        key_rows = jnp.concatenate([pool[table_row].reshape(prefix_tokens, LAT), latent], axis=0)
        scores = jnp.einsum('nhc,kc->nhk', query_rows.astype(jnp.float32), key_rows.astype(jnp.float32)) * scale
        key_pos = jnp.arange(prefix_tokens + NEW, dtype=jnp.int32)
        token_ids = jnp.arange(NEW, dtype=jnp.int32)
        allowed = jnp.where(key_pos[None, :] < prefix_tokens, key_pos[None, :] < length, key_pos[None, :] - prefix_tokens <= token_ids[:, None])
        scores = jnp.where(allowed[:, None, :], scores, masked_value)
        row_max = lax.optimization_barrier(jnp.max(scores, axis=-1, keepdims=True))
        expo = jnp.exp(scores - row_max)
        weights = (expo / lax.optimization_barrier(jnp.sum(expo, axis=-1, keepdims=True))).astype(jnp.bfloat16)
        context = jnp.einsum('nhk,kc->nhc', weights.astype(jnp.float32), key_rows[:, :KVR].astype(jnp.float32)).astype(jnp.bfloat16)
        head_out = jnp.einsum('nhc,chv->nhv', context.astype(jnp.float32), value_up).astype(jnp.bfloat16)
        return (head_out.reshape(NEW, H * VDIM), latent)
    head_outs, latents = lax.map(one_request, (hidden.reshape(N_GROUP, NEW, D), q_latent.reshape(N_GROUP, NEW, QR), page_table, prefix_len))
    request_of_group = jnp.zeros((N_GROUP,), jnp.int32).at[decode_owner].set(jnp.arange(N_GROUP, dtype=jnp.int32))
    decode_pages = latents[request_of_group].reshape(N_GROUP * NEW, LAT)
    return (head_outs.reshape(N_GROUP * NEW, H * VDIM), decode_pages)
```

```python
import functools

import jax
import jax.numpy as jnp
from jax import lax
from jax.experimental import pallas as pl
from jax.experimental.pallas import tpu as pltpu
from jax.sharding import PartitionSpec as P

NOPE = 128
ROPE = 64
VDIM = 128
KVR = 512
CAP = 2
LAT = KVR + ROPE
WIDE = 640
HALF = ROPE // 2

rope_base = 50000.0
masked_value = -1e30
softmax_scale = float(NOPE + ROPE) ** (-0.5)
log2_scale = softmax_scale * 1.4426950408889634

MIB = 1 << 20
bf16 = jnp.bfloat16
f32 = jnp.float32


def vmem():
    return pl.BlockSpec(memory_space=pltpu.VMEM)


def smem():
    return pl.BlockSpec(memory_space=pltpu.SMEM)


def angle_tables(positions):
    frequency = rope_base ** (-2.0 * jnp.arange(HALF, dtype=f32) / ROPE)
    return positions.astype(f32), frequency


def query_kernel(ql_ref, wq_ref, wk_ref, cos_ref, sin_ref, out_ref):
    q = jnp.dot(ql_ref[...], wq_ref[...], preferred_element_type=f32)
    qt = q.T
    cosine = cos_ref[...]
    sine = sin_ref[...]
    tokens = qt.shape[1]
    for h in range(2):
        base = h * (NOPE + ROPE)
        nope = qt[base:base + NOPE].astype(bf16)
        first = qt[base + NOPE:base + NOPE + HALF]
        second = qt[base + NOPE + HALF:base + NOPE + ROPE]
        absorbed = jnp.dot(wk_ref[:, h * NOPE:(h + 1) * NOPE], nope, preferred_element_type=f32)
        out_ref[h, :KVR, :] = absorbed.astype(bf16)
        out_ref[h, KVR:KVR + HALF, :] = (first * cosine - second * sine).astype(bf16)
        out_ref[h, KVR + HALF:LAT, :] = (second * cosine + first * sine).astype(bf16)
        row = lax.broadcasted_iota(jnp.int32, (WIDE - LAT, tokens), 0)
        out_ref[h, LAT:, :] = jnp.where(row == 0, 1.0, 0.0).astype(bf16)


def make_queries(q_latent, w_q_b, w_key_up, cos_t, sin_t):
    tokens, rank = q_latent.shape
    heads = w_key_up.shape[1] // NOPE
    return pl.pallas_call(
        query_kernel,
        grid=(heads // 2,),
        in_specs=[
            pl.BlockSpec((tokens, rank), lambda i: (0, 0)),
            pl.BlockSpec((rank, 2 * (NOPE + ROPE)), lambda i: (0, i)),
            pl.BlockSpec((KVR, 2 * NOPE), lambda i: (0, i)),
            pl.BlockSpec((HALF, tokens), lambda i: (0, 0)),
            pl.BlockSpec((HALF, tokens), lambda i: (0, 0)),
        ],
        out_specs=pl.BlockSpec((2, WIDE, tokens), lambda i: (i, 0, 0)),
        out_shape=jax.ShapeDtypeStruct((heads, WIDE, tokens), bf16),
        compiler_params=pltpu.CompilerParams(vmem_limit_bytes=32 * MIB),
        cost_estimate=pl.CostEstimate(flops=2 * tokens * rank * heads * 192 + 2 * tokens * KVR * heads * 128,
                                      bytes_accessed=8 * MIB, transcendentals=0),
        name="queries",
    )(q_latent, w_q_b, w_key_up, cos_t, sin_t)


def combine_kernel(y_ref, a_ref, b_ref, own_ref, up_ref, down_ref, far_ref):
    y = y_ref[0]
    rows = own_ref.shape[0]

    def part(d):
        start = pl.multiple_of(lax.rem(y + d, 4) * rows, rows)
        return a_ref[pl.ds(start, rows), :].astype(f32) + b_ref[pl.ds(start, rows), :].astype(f32)

    own_ref[...] = part(0)
    up_ref[...] = part(1).astype(bf16)
    far_ref[...] = part(2).astype(bf16)
    down_ref[...] = part(3).astype(bf16)


def combine(y, a, b):
    rows = a.shape[0] // 4
    return pl.pallas_call(
        combine_kernel,
        in_specs=[smem(), vmem(), vmem()],
        out_specs=[vmem()] * 4,
        out_shape=[jax.ShapeDtypeStruct((rows, LAT), f32)] + [jax.ShapeDtypeStruct((rows, LAT), bf16)] * 3,
        cost_estimate=pl.CostEstimate(flops=a.size, bytes_accessed=8 * a.size, transcendentals=0),
        name="combine",
    )(y, a, b)


def finish_kernel(own_ref, a_ref, b_ref, c_ref, gain_ref, cos_ref, sin_ref, out_ref):
    total = (own_ref[...] + a_ref[...].astype(f32)) + (b_ref[...].astype(f32) + c_ref[...].astype(f32))
    nope = total[:, :KVR]
    mean_square = jnp.mean(nope * nope, axis=-1, keepdims=True)
    out_ref[:, :KVR] = (nope * lax.rsqrt(mean_square + 1e-06) * gain_ref[...]).astype(bf16)
    first = total[:, KVR:KVR + HALF]
    second = total[:, KVR + HALF:LAT]
    cosine = cos_ref[...]
    sine = sin_ref[...]
    rotated = jnp.concatenate([first * cosine - second * sine, second * cosine + first * sine], axis=-1)
    out_ref[:, KVR:LAT] = rotated.astype(bf16)


def finish(own, a, b, c, gain, cosine, sine):
    return pl.pallas_call(
        finish_kernel,
        in_specs=[vmem()] * 7,
        out_specs=vmem(),
        out_shape=jax.ShapeDtypeStruct(own.shape, bf16),
        cost_estimate=pl.CostEstimate(flops=8 * own.size, bytes_accessed=12 * own.size, transcendentals=0),
        name="finish",
    )(own, a, b, c, gain, cosine, sine)


def attention_kernel(blocks, news, first, last, *refs):
    refs = list(refs)
    info_ref = refs.pop(0)
    pos_ref = refs.pop(0)
    qt_ref = refs.pop(0)
    key_refs = [refs.pop(0) for _ in range(blocks)]
    new_refs = [refs.pop(0) for _ in range(news)]
    if not first:
        m_in, l_in, acc_in = refs.pop(0), refs.pop(0), refs.pop(0)
    if last:
        wv_ref = refs.pop(0)
        out_ref = refs.pop(0)
    else:
        m_out, l_out, acc_out = refs.pop(0), refs.pop(0), refs.pop(0)
    keys, values_t = refs
    heads = qt_ref.shape[0]
    tokens = qt_ref.shape[2]
    rows = pos_ref.shape[0]
    lane = lax.broadcasted_iota(jnp.int32, (rows, WIDE - LAT), 1)
    for b in range(blocks):
        here = slice(b * rows, (b + 1) * rows)
        ref = key_refs[b]
        nope = ref[:, :KVR]
        keys[here, :KVR] = nope
        keys[here, KVR:LAT] = ref[:, KVR:LAT]
        out_of_range = jnp.logical_and(pos_ref[...] >= info_ref[b], lane == 0)
        keys[here, LAT:] = jnp.where(out_of_range, masked_value, 0.0).astype(bf16)
        values_t[:, here] = nope.T
    prefix = blocks * rows
    total = prefix
    causal = []
    for b in range(news):
        ref = new_refs[b]
        n = ref.shape[0]
        here = slice(total, total + n)
        nope = ref[...][:, :KVR]
        keys[here, :KVR] = nope
        keys[here, KVR:LAT] = ref[:, KVR:LAT]
        keys[here, LAT:] = jnp.zeros((n, WIDE - LAT), bf16)
        key_token = info_ref[blocks + b] + lax.broadcasted_iota(jnp.int32, (n, tokens), 0)
        causal.append(key_token <= lax.broadcasted_iota(jnp.int32, (n, tokens), 1))
        total += n
    if news:
        values_t[:, prefix:total] = keys[prefix:total, :KVR].T
        allowed = jnp.concatenate(causal, axis=0)
    for h in range(heads):
        s = jnp.dot(keys[...], qt_ref[h], preferred_element_type=f32)
        if news:
            s = jnp.concatenate([s[:prefix], jnp.where(allowed, s[prefix:], masked_value)], axis=0)
        top = jnp.max(s, axis=0, keepdims=True)
        if not first:
            old = m_in[h:h + 1, :]
            top = jnp.maximum(top, old)
        p = jnp.exp2((s - top) * log2_scale)
        norm = jnp.sum(p, axis=0, keepdims=True)
        acc = jnp.dot(values_t[...], p.astype(bf16), preferred_element_type=f32)
        if not first:
            alpha = jnp.exp2((old - top) * log2_scale)
            norm = norm + l_in[h:h + 1, :] * alpha
            acc = acc + acc_in[h] * alpha
        if last:
            context = (acc / norm).astype(bf16)
            head_out = lax.dot_general(
                wv_ref[:, h * VDIM:(h + 1) * VDIM], context, (((0,), (0,)), ((), ())), preferred_element_type=f32
            )
            out_ref[:, h * VDIM:(h + 1) * VDIM] = head_out.T.astype(bf16)
        else:
            m_out[h:h + 1, :] = top
            l_out[h:h + 1, :] = norm
            acc_out[h] = acc


def attention(info, pos, qt, key_blocks, new_blocks, state, w_value_up):
    heads, _, tokens = qt.shape
    first = state is None
    last = w_value_up is not None
    total = sum(b.shape[0] for b in key_blocks) + sum(b.shape[0] for b in new_blocks)
    args = [info, pos, qt, *key_blocks, *new_blocks]
    if not first:
        args += list(state)
    if last:
        args.append(w_value_up)
        out_shape = jax.ShapeDtypeStruct((tokens, heads * VDIM), bf16)
        out_specs = vmem()
    else:
        out_shape = [
            jax.ShapeDtypeStruct((heads, tokens), f32),
            jax.ShapeDtypeStruct((heads, tokens), f32),
            jax.ShapeDtypeStruct((heads, KVR, tokens), f32),
        ]
        out_specs = [vmem()] * 3
    return pl.pallas_call(
        functools.partial(attention_kernel, len(key_blocks), len(new_blocks), first, last),
        in_specs=[smem()] + [vmem()] * (len(args) - 1),
        out_specs=out_specs,
        out_shape=out_shape,
        scratch_shapes=[pltpu.VMEM((total, WIDE), bf16), pltpu.VMEM((KVR, total), bf16)],
        compiler_params=pltpu.CompilerParams(vmem_limit_bytes=40 * MIB),
        cost_estimate=pl.CostEstimate(flops=2 * heads * tokens * total * (WIDE + KVR), bytes_accessed=8 * MIB,
                                      transcendentals=heads * tokens * total),
        name="attention",
    )(*args)


def shards(
    hidden,
    w_kv_a,
    kv_gain,
    q_latent,
    w_q_b,
    w_key_up,
    w_value_up,
    pool,
    page_table,
    prefix_len,
    decode_owner,
):
    groups = lax.axis_size("group")
    group_index = lax.axis_index("group")
    tensor_index = lax.axis_index("tensor")
    y = tensor_index // 2
    core = tensor_index % 2
    new_tokens = hidden.shape[0]
    slot_count = pool.shape[0]
    page_rows = pool.shape[1]
    max_pages = page_table.shape[1]
    my_length = prefix_len[group_index]
    group_ids = jnp.arange(groups, dtype=jnp.int32)

    def tensor_permute(x, step):
        return lax.ppermute(x, "tensor", [(i, step(i)) for i in range(8)])

    up = lambda i: (i + 2) % 8
    down = lambda i: (i - 2) % 8
    far = lambda i: (i + 4) % 8
    other = lambda i: i ^ 1

    owner_table = page_table // slot_count
    page_ids = jnp.arange(max_pages, dtype=jnp.int32)
    code = page_ids[None, :] * slot_count + page_table % slot_count
    mine = owner_table == group_index
    first_code = jnp.min(jnp.where(mine, code, max_pages * slot_count), axis=1)
    last_code = jnp.max(jnp.where(mine, code, -1), axis=1)
    picked = jnp.stack([first_code, last_code], axis=1) % slot_count
    outgoing = pool[picked]
    incoming = lax.all_to_all(outgoing, "group", split_axis=0, concat_axis=0, tiled=True)
    own_block = incoming.reshape(groups * CAP * page_rows, LAT)

    my_owners = owner_table[group_index]
    owned = my_owners[None, :] == group_ids[:, None]
    first_page = jnp.min(jnp.where(owned, page_ids[None, :], max_pages), axis=1)
    last_page = jnp.max(jnp.where(owned, page_ids[None, :], -1), axis=1)
    pages = jnp.stack([first_page, last_page], axis=1)
    row_ids = jnp.arange(page_rows, dtype=jnp.int32)
    pos = (pages[:, :, None] * (page_rows * 8) + row_ids).reshape(-1, 1)

    frequency = rope_base ** (-2.0 * jnp.arange(HALF, dtype=f32) / ROPE)
    positions = (my_length + jnp.arange(new_tokens, dtype=jnp.int32)).astype(f32)
    angles_t = frequency[:, None] * positions[None, :]
    chip_rows = new_tokens // 4
    chip_positions = (my_length + y * chip_rows + jnp.arange(chip_rows, dtype=jnp.int32)).astype(f32)
    angles = chip_positions[:, None] * frequency[None, :]
    partial_sum = jnp.dot(hidden, w_kv_a, preferred_element_type=f32).astype(bf16)
    partner_sum = tensor_permute(partial_sum, other)
    own, to_up, to_down, to_far = combine(y[None], partial_sum, partner_sum)
    from_down = tensor_permute(to_up, up)
    from_up = tensor_permute(to_down, down)
    from_far = tensor_permute(to_far, far)
    latent = finish(own, from_down, from_up, from_far, kv_gain[None, :], jnp.cos(angles), jnp.sin(angles))
    latents = [latent, tensor_permute(latent, up), tensor_permute(latent, down), tensor_permute(latent, far)]
    new_starts = [y, (y + 3) % 4, (y + 1) % 4, (y + 2) % 4]

    share_rows = new_tokens // 8
    share = lax.dynamic_slice_in_dim(latent, core * share_rows, share_rows, 0)
    spread = lax.all_to_all(share[:, None, :], "group", 0, 0, tiled=True)
    source = jnp.sum(jnp.where(decode_owner[None, :] == group_ids[:, None], group_ids[None, :], 0), axis=1)
    decode_pages = lax.all_to_all(spread[source], "group", 0, 0, tiled=True).reshape(share_rows, LAT)

    qt = make_queries(q_latent, w_q_b, w_key_up, jnp.cos(angles_t), jnp.sin(angles_t))

    block_up = tensor_permute(own_block, up)
    block_down = tensor_permute(own_block, down)
    block_far = tensor_permute(own_block, far)
    block_other = tensor_permute(own_block, other)
    block_up_other = tensor_permute(block_up, other)
    block_down_other = tensor_permute(block_down, other)
    block_far_other = tensor_permute(block_far, other)

    def limit(source_tensor):
        return my_length - page_rows * source_tensor

    t = tensor_index
    info1 = jnp.stack([limit(t), limit(t ^ 1)] + [s * chip_rows for s in new_starts])
    state = attention(info1, pos, qt, [own_block, block_other], latents, None, None)
    below, above, across = (t + 6) % 8, (t + 2) % 8, (t + 4) % 8
    info2 = jnp.stack([limit(below), limit(below ^ 1), limit(above), limit(above ^ 1)])
    state = attention(info2, pos, qt, [block_up, block_up_other, block_down, block_down_other], [], state, None)
    info3 = jnp.stack([limit(across), limit(across ^ 1)])
    attn_out = attention(info3, pos, qt, [block_far, block_far_other], [], state, w_value_up)
    return (attn_out, decode_pages)


def solution(mesh):
    return jax.shard_map(
        shards,
        mesh=mesh,
        in_specs=(
            P("group", "tensor"),
            P("tensor", None),
            P(),
            P("group", None),
            P(None, "tensor"),
            P(None, "tensor"),
            P(None, "tensor"),
            P("group", "tensor", None),
            P(),
            P(),
            P(),
        ),
        out_specs=(P("group", "tensor"), P(("group", "tensor"), None)),
        check_vma=False,
    )
```

```python
import functools

import jax
import jax.numpy as jnp
from jax import lax
from jax.experimental import pallas as pl
from jax.experimental.pallas import tpu as pltpu
from jax.sharding import PartitionSpec as P

NOPE = 128
ROPE = 64
VDIM = 128
KVR = 512
CAP = 2
LAT = KVR + ROPE
QWIDE = 256
HALF = ROPE // 2

rope_base = 50000.0
masked_value = -1e30
softmax_scale = float(NOPE + ROPE) ** (-0.5)
log2_scale = softmax_scale * 1.4426950408889634

MIB = 1 << 20
bf16 = jnp.bfloat16
f32 = jnp.float32


def vmem():
    return pl.BlockSpec(memory_space=pltpu.VMEM)


def hbm():
    return pl.BlockSpec(memory_space=pltpu.HBM)


def anywhere():
    return pl.BlockSpec(memory_space=pl.ANY)


def smem():
    return pl.BlockSpec(memory_space=pltpu.SMEM)


def select_kernel(table_ref, pool_ref, out_ref, pos_ref):
    group = lax.axis_index("group")
    page_rows, _, slot_count = pool_ref.shape
    requests, max_pages = table_ref.shape
    shift = slot_count.bit_length() - 1
    rows = requests * CAP * page_rows
    table = table_ref[...]
    page = lax.broadcasted_iota(jnp.int32, table.shape, 1)
    code = page * slot_count + (table & (slot_count - 1))
    mine = (table >> shift) == group
    first = jnp.min(jnp.where(mine, code, max_pages * slot_count), axis=1, keepdims=True) & (slot_count - 1)
    last = jnp.max(jnp.where(mine, code, 0), axis=1, keepdims=True) & (slot_count - 1)
    shape = (requests, CAP * page_rows, slot_count)
    part = lax.broadcasted_iota(jnp.int32, shape, 1)
    slot = lax.broadcasted_iota(jnp.int32, shape, 2)
    first = jnp.broadcast_to(first[:, :, None], shape)
    last = jnp.broadcast_to(last[:, :, None], shape)
    hit = slot == jnp.where(part < page_rows, first, last)
    total = None
    for u in range(page_rows):
        pick = jnp.where(jnp.logical_and(hit, part % page_rows == u), 1.0, 0.0).reshape(rows, slot_count).astype(bf16)
        term = lax.dot_general(pick, pool_ref[u], (((1,), (1,)), ((), ())), preferred_element_type=f32)
        total = term if total is None else total + term
    out_ref[...] = total.astype(bf16)
    owners = table_ref[pl.ds(group, 1), :] >> shift
    row = lax.broadcasted_iota(jnp.int32, (rows, max_pages), 0)
    column = lax.broadcasted_iota(jnp.int32, (rows, max_pages), 1)
    held = owners == row // (CAP * page_rows)
    first_page = jnp.min(jnp.where(held, column, max_pages), axis=1, keepdims=True)
    last_page = jnp.max(jnp.where(held, column, 0), axis=1, keepdims=True)
    one_row = lax.broadcasted_iota(jnp.int32, (rows, 1), 0)
    at = jnp.where((one_row // page_rows) % CAP == 0, first_page, last_page)
    pos_ref[...] = at * (page_rows * 8) + one_row % page_rows


def select(page_table, pool):
    rows = page_table.shape[0] * CAP * pool.shape[1]
    return pl.pallas_call(
        select_kernel,
        in_specs=[vmem(), vmem()],
        out_specs=[vmem(), vmem()],
        out_shape=[jax.ShapeDtypeStruct((rows, LAT), bf16), jax.ShapeDtypeStruct((rows, 1), jnp.int32)],
        cost_estimate=pl.CostEstimate(flops=8 * rows * 128 * LAT, bytes_accessed=1000000, transcendentals=0),
        name="select",
    )(page_table, jnp.transpose(pool, (1, 2, 0)))


def project_kernel(x_ref, w_ref, out_ref):
    total = lax.dot_general(x_ref[...], w_ref[...], (((1,), (1,)), ((), ())), preferred_element_type=f32)
    out_ref[...] = total.astype(bf16)


def project(x, w):
    return pl.pallas_call(
        project_kernel,
        in_specs=[vmem(), vmem()],
        out_specs=vmem(),
        out_shape=jax.ShapeDtypeStruct((x.shape[0], w.shape[0]), bf16),
        cost_estimate=pl.CostEstimate(flops=2 * x.size * w.shape[0], bytes_accessed=2 * (x.size + w.size),
                                      transcendentals=0),
        name="project",
    )(x, w)


def rotary(frequency, length, first_token, tokens):
    token = first_token + lax.broadcasted_iota(jnp.int32, (HALF, tokens), 1)
    angles = frequency * (length + token).astype(f32)
    return jnp.cos(angles), jnp.sin(angles)


def query_kernel(length_ref, frequency_ref, ql_ref, wq_hbm, out_ref, wq_ref, sems):
    heads, _, tokens = out_ref.shape
    pair_width = 2 * (NOPE + ROPE)
    copies = []
    for pair in range(heads // 2):
        columns = pl.ds(pair * pair_width, pair_width)
        copy = pltpu.make_async_copy(wq_hbm.at[:, columns], wq_ref.at[pair], sems.at[pair])
        copy.start()
        copies.append(copy)
    cosine, sine = rotary(frequency_ref[...], length_ref[lax.axis_index("group")], 0, tokens)
    row = lax.broadcasted_iota(jnp.int32, (QWIDE - NOPE - ROPE, tokens), 0)
    tail = jnp.where(row == 0, 1.0, 0.0).astype(bf16)
    for pair in range(heads // 2):
        copies[pair].wait()
        qt = jnp.dot(ql_ref[...], wq_ref[pair], preferred_element_type=f32).T
        for i in range(2):
            h = 2 * pair + i
            base = i * (NOPE + ROPE)
            first = qt[base + NOPE:base + NOPE + HALF]
            second = qt[base + NOPE + HALF:base + NOPE + ROPE]
            out_ref[h, :NOPE, :] = qt[base:base + NOPE].astype(bf16)
            out_ref[h, NOPE:NOPE + HALF, :] = (first * cosine - second * sine).astype(bf16)
            out_ref[h, NOPE + HALF:NOPE + ROPE, :] = (second * cosine + first * sine).astype(bf16)
            out_ref[h, NOPE + ROPE:, :] = tail


def make_queries(prefix_len, frequency, q_latent, w_q_b):
    tokens, rank = q_latent.shape
    heads = w_q_b.shape[1] // (NOPE + ROPE)
    return pl.pallas_call(
        query_kernel,
        in_specs=[smem(), vmem(), vmem(), hbm()],
        out_specs=vmem(),
        out_shape=jax.ShapeDtypeStruct((heads, QWIDE, tokens), bf16),
        scratch_shapes=[
            pltpu.VMEM((heads // 2, rank, 2 * (NOPE + ROPE)), bf16),
            pltpu.SemaphoreType.DMA((heads // 2,)),
        ],
        compiler_params=pltpu.CompilerParams(vmem_limit_bytes=24 * MIB),
        cost_estimate=pl.CostEstimate(flops=2 * tokens * rank * heads * 192, bytes_accessed=6 * MIB, transcendentals=0),
        name="queries",
    )(prefix_len, frequency, q_latent, w_q_b)


def combine_kernel(a_ref, b_ref, own_ref, up_ref, down_ref, far_ref):
    y = lax.axis_index("tensor") // 2
    rows = own_ref.shape[0]

    def part(d):
        start = pl.multiple_of(lax.rem(y + d, 4) * rows, rows)
        return a_ref[pl.ds(start, rows), :].astype(f32) + b_ref[pl.ds(start, rows), :].astype(f32)

    own_ref[...] = part(0)
    up_ref[...] = part(1).astype(bf16)
    far_ref[...] = part(2).astype(bf16)
    down_ref[...] = part(3).astype(bf16)


def combine(a, b):
    rows = a.shape[0] // 4
    return pl.pallas_call(
        combine_kernel,
        in_specs=[vmem(), vmem()],
        out_specs=[vmem()] * 4,
        out_shape=[jax.ShapeDtypeStruct((rows, LAT), f32)] + [jax.ShapeDtypeStruct((rows, LAT), bf16)] * 3,
        cost_estimate=pl.CostEstimate(flops=a.size, bytes_accessed=8 * a.size, transcendentals=0),
        name="combine",
    )(a, b)


def finish_kernel(length_ref, frequency_ref, own_ref, a_ref, b_ref, c_ref, gain_ref, _, out_ref, share_ref):
    total = (own_ref[...] + a_ref[...].astype(f32)) + (b_ref[...].astype(f32) + c_ref[...].astype(f32))
    rows = total.shape[0]
    nope = total[:, :KVR]
    mean_square = jnp.mean(nope * nope, axis=-1, keepdims=True)
    turned = total[:, KVR:LAT].T
    first = turned[:HALF]
    second = turned[HALF:]
    tensor = lax.axis_index("tensor")
    length = length_ref[lax.axis_index("group")]
    cosine, sine = rotary(frequency_ref[...], length, tensor // 2 * rows, rows)
    rotated = jnp.concatenate([first * cosine - second * sine, second * cosine + first * sine], axis=0).T
    out_ref[:, :KVR] = (nope * lax.rsqrt(mean_square + 1e-06) * gain_ref[...]).astype(bf16)
    out_ref[:, KVR:LAT] = rotated.astype(bf16)
    half = rows // 2
    core = lax.rem(tensor, 2)
    share_ref[...] = out_ref[pl.ds(pl.multiple_of(core * half, half), half), :]


def finish(prefix_len, frequency, own, a, b, c, gain, earlier):
    rows = own.shape[0]
    return pl.pallas_call(
        finish_kernel,
        in_specs=[smem()] + [vmem()] * 6 + [anywhere()],
        out_specs=[vmem(), vmem()],
        out_shape=[jax.ShapeDtypeStruct(own.shape, bf16), jax.ShapeDtypeStruct((rows // 2, LAT), bf16)],
        cost_estimate=pl.CostEstimate(flops=8 * own.size, bytes_accessed=12 * own.size, transcendentals=0),
        name="finish",
    )(prefix_len, frequency, own, a, b, c, gain, earlier)


def address_kernel(owner_ref, *refs):
    in_refs, out_ref = refs[:4], refs[4]
    group = lax.axis_index("group")
    x = lax.rem(group, 4)
    out_ref[...] = jnp.zeros_like(out_ref)
    for turn in range(4):
        owner = owner_ref[group - x + lax.rem(x - turn + 4, 4)]

        @pl.when(lax.rem(owner, 4) == x)
        def _():
            out_ref[owner // 4] = in_refs[turn][...]


def address(decode_owner, shares):
    rows = shares[0].shape[0]
    return pl.pallas_call(
        address_kernel,
        in_specs=[smem()] + [vmem()] * 4,
        out_specs=vmem(),
        out_shape=jax.ShapeDtypeStruct((8, rows, LAT), bf16),
        cost_estimate=pl.CostEstimate(flops=1000, bytes_accessed=20 * rows * LAT, transcendentals=0),
        name="address",
    )(decode_owner, *shares)


def pick_kernel(owner_ref, in_ref, _, out_ref, sem):
    group = lax.axis_index("group")
    request = jnp.int32(0)
    for r in range(owner_ref.shape[0]):
        request = request + jnp.where(owner_ref[r] == group, r, 0)
    copy = pltpu.make_async_copy(in_ref.at[request // 4], out_ref, sem)
    copy.start()
    copy.wait()


def pick(decode_owner, arrived, earlier):
    rows = arrived.shape[1]
    return pl.pallas_call(
        pick_kernel,
        in_specs=[smem(), anywhere(), anywhere()],
        out_specs=vmem(),
        out_shape=jax.ShapeDtypeStruct((rows, LAT), bf16),
        scratch_shapes=[pltpu.SemaphoreType.DMA],
        cost_estimate=pl.CostEstimate(flops=1000, bytes_accessed=4 * rows * LAT, transcendentals=0),
        name="pick",
    )(decode_owner, arrived, earlier)


def after(x, token):
    return pl.pallas_call(
        lambda x_ref, token_ref, out_ref: None,
        in_specs=[anywhere(), anywhere()],
        out_specs=anywhere(),
        out_shape=jax.ShapeDtypeStruct(x.shape, x.dtype),
        input_output_aliases={0: 0},
        cost_estimate=pl.CostEstimate(flops=0, bytes_accessed=0, transcendentals=0),
        name="after",
    )(x, token)


def attention_kernel(turns, length_ref, pos_ref, qt_ref, wk_hbm, wv_hbm, cached_ref, *refs):
    refs = list(refs)
    new_refs = [refs.pop(0) for _ in turns]
    out_ref, tails, keys, values, scores, weights, landed, fresh, wk_ref, wv_ref, sems, w_sems = refs
    heads, _, tokens = qt_ref.shape
    rows = pos_ref.shape[0]
    blocks = landed.shape[0]
    tiles = blocks + 1
    tensor = lax.axis_index("tensor")
    length = length_ref[lax.axis_index("group")]
    ups = []
    for pair in range(heads // 2):
        columns = pl.ds(pair * 256, 256)
        for i, (source, target) in enumerate(((wk_hbm, wk_ref), (wv_hbm, wv_ref))):
            copy = pltpu.make_async_copy(source.at[:, columns], target.at[:, columns], w_sems.at[2 * pair + i])
            copy.start()
            ups.append(copy)
    copies = []
    for b in range(blocks):
        copy = pltpu.make_async_copy(cached_ref.at[pl.ds(b * rows, rows), :], landed.at[b], sems.at[b])
        copy.start()
        copies.append(copy)
    latents = [landed.at[b] for b in range(blocks)] + [fresh]
    causal = []
    for b, turn in enumerate(turns):
        n = new_refs[b].shape[0]
        fresh[b * n:(b + 1) * n, :] = new_refs[b][...]
        key_token = lax.rem(tensor // 2 + turn, 4) * n + lax.broadcasted_iota(jnp.int32, (n, tokens), 0)
        causal.append(key_token <= lax.broadcasted_iota(jnp.int32, (n, tokens), 1))
    allowed = jnp.concatenate(causal, axis=0)
    lane = lax.broadcasted_iota(jnp.int32, (rows, 128 - ROPE), 1)

    def stage(j):
        here = slice(j * rows, (j + 1) * rows)
        if j < blocks:
            copies[j].wait()
            out_of_range = jnp.logical_and(pos_ref[...] >= length - 4 * j, lane == 0)
            tails[here, ROPE:] = jnp.where(out_of_range, masked_value, 0.0).astype(bf16)
        else:
            tails[here, ROPE:] = jnp.zeros((rows, 128 - ROPE), bf16)
        tails[here, :ROPE] = latents[j][:, KVR:LAT]

    def project_up(pair, j):
        here = slice(j * rows, (j + 1) * rows)
        nope = latents[j][:, :KVR]
        columns = slice(pair * 256, (pair + 1) * 256)
        k = jnp.dot(nope, wk_ref[:, columns], preferred_element_type=f32).astype(bf16)
        v = lax.dot_general(
            wv_ref[:, columns], nope, (((0,), (1,)), ((), ())), preferred_element_type=f32
        ).astype(bf16)
        for i in range(2):
            slot = 2 * (pair % 2) + i
            keys[slot, here, :NOPE] = k[:, i * NOPE:(i + 1) * NOPE]
            keys[slot, here, NOPE:] = tails[here, :]
            values[slot, :, here] = v[i * VDIM:(i + 1) * VDIM]

    def score(h, j):
        here = slice(j * rows, (j + 1) * rows)
        s = jnp.dot(keys[h % 4, here], qt_ref[h], preferred_element_type=f32)
        if j >= blocks:
            s = jnp.where(allowed, s, masked_value)
        scores[h % 2, here] = s
        return jnp.max(s, axis=0, keepdims=True)

    def weigh(h, j, top):
        here = slice(j * rows, (j + 1) * rows)
        p = jnp.exp2((scores[h % 2, here] - top) * log2_scale)
        weights[h % 2, here] = p.astype(bf16)
        return jnp.sum(p, axis=0, keepdims=True)

    order = [blocks] + list(range(blocks))
    tops = []
    for copy in ups[:2]:
        copy.wait()
    for j in order:
        stage(j)
        project_up(0, j)
        tops.append(score(0, j))
    for h in range(heads):
        top = functools.reduce(jnp.maximum, tops)
        tops = []
        norms = []
        if h % 2 == 0 and h + 2 < heads:
            for copy in ups[h + 2:h + 4]:
                copy.wait()
        for i, j in enumerate(order):
            if h // 2 * 2 + 2 < heads and i % 2 == h % 2:
                project_up(h // 2 + 1, j)
            if h + 1 < heads:
                tops.append(score(h + 1, j))
            norms.append(weigh(h, j, top))
        norm = functools.reduce(jnp.add, norms)
        acc = jnp.dot(values[h % 4], weights[h % 2], preferred_element_type=f32)
        out_ref[:, h * VDIM:(h + 1) * VDIM] = (acc / norm).T.astype(bf16)


def attention(prefix_len, pos, qt, w_key_up, w_value_up, cached, turns, new_blocks):
    heads, _, tokens = qt.shape
    rows = pos.shape[0]
    blocks = cached.shape[0] // rows
    total = rows * (blocks + 1)
    return pl.pallas_call(
        functools.partial(attention_kernel, turns),
        in_specs=[smem()] + [vmem()] * 2 + [hbm()] * 3 + [vmem()] * len(new_blocks),
        out_specs=vmem(),
        out_shape=jax.ShapeDtypeStruct((tokens, heads * VDIM), bf16),
        scratch_shapes=[
            pltpu.VMEM((total, 128), bf16),
            pltpu.VMEM((4, total, QWIDE), bf16),
            pltpu.VMEM((4, VDIM, total), bf16),
            pltpu.VMEM((2, total, tokens), f32),
            pltpu.VMEM((2, total, tokens), bf16),
            pltpu.VMEM((blocks, rows, LAT), bf16),
            pltpu.VMEM((rows, LAT), bf16),
            pltpu.VMEM(w_key_up.shape, bf16),
            pltpu.VMEM(w_value_up.shape, bf16),
            pltpu.SemaphoreType.DMA((blocks,)),
            pltpu.SemaphoreType.DMA((heads,)),
        ],
        compiler_params=pltpu.CompilerParams(vmem_limit_bytes=32 * MIB),
        cost_estimate=pl.CostEstimate(flops=4 * heads * tokens * total * 512, bytes_accessed=4 * MIB,
                                      transcendentals=heads * tokens * total),
        name="attention",
    )(prefix_len, pos, qt, w_key_up, w_value_up, cached, *new_blocks)


def shards(
    hidden,
    w_kv_a,
    kv_gain,
    q_latent,
    w_q_b,
    w_key_up,
    w_value_up,
    pool,
    page_table,
    prefix_len,
    decode_owner,
):

    def tensor_permute(x, step):
        return lax.ppermute(x, "tensor", [(i, step(i)) for i in range(8)])

    up = lambda i: (i + 2) % 8
    down = lambda i: (i - 2) % 8
    far = lambda i: (i + 4) % 8
    other = lambda i: i ^ 1

    outgoing, pos = select(page_table, pool)
    outgoing = outgoing.reshape(page_table.shape[0], -1, LAT)
    incoming = lax.all_to_all(outgoing, "group", split_axis=0, concat_axis=0, tiled=True)
    own_block = incoming.reshape(pos.shape[0], LAT)

    frequency = (rope_base ** (-2.0 * jnp.arange(HALF, dtype=f32) / ROPE))[:, None]
    qt = make_queries(prefix_len, frequency, q_latent, w_q_b)

    partial_sum = project(hidden, w_kv_a.T)
    partner_sum = tensor_permute(partial_sum, other)
    own, to_up, to_down, to_far = combine(partial_sum, partner_sum)
    from_down = tensor_permute(to_up, up)
    from_up = tensor_permute(to_down, down)
    from_far = tensor_permute(to_far, far)
    latent, share = finish(prefix_len, frequency, own, from_down, from_up, from_far, kv_gain[None, :], qt)
    latents = [latent, tensor_permute(latent, up), tensor_permute(latent, down), tensor_permute(latent, far)]

    def x_permute(turn):
        return lax.ppermute(share, "group", [(i, i // 4 * 4 + (i + turn) % 4) for i in range(32)])

    columns = [[4 * z + x for z in range(8)] for x in range(4)]
    addressed = address(decode_owner, [share, x_permute(1), x_permute(2), x_permute(3)])
    arrived = lax.all_to_all(addressed, "group", 0, 0, tiled=True, axis_index_groups=columns)

    own_block = after(own_block, own)
    cached = lax.all_gather(own_block, "tensor", axis=0, tiled=True)
    attn_out = attention(prefix_len, pos, qt, w_key_up, w_value_up, cached, (0, 3, 1, 2), latents)
    decode_pages = pick(decode_owner, arrived, attn_out)
    return (attn_out, decode_pages)


def solution(mesh):
    return jax.shard_map(
        shards,
        mesh=mesh,
        in_specs=(
            P("group", "tensor"),
            P("tensor", None),
            P(),
            P("group", None),
            P(None, "tensor"),
            P(None, "tensor"),
            P(None, "tensor"),
            P("group", "tensor", None),
            P(),
            P(),
            P(),
        ),
        out_specs=(P("group", "tensor"), P(("group", "tensor"), None)),
        check_vma=False,
    )
```

```python
import functools

import jax
import jax.numpy as jnp
import numpy as np
from jax import lax
from jax.experimental import pallas as pl
from jax.experimental.pallas import tpu as pltpu
from jax.sharding import PartitionSpec as P

NOPE = 128
ROPE = 64
VDIM = 128
KVR = 512
CAP = 2
LAT = KVR + ROPE
QWIDE = 256
WIDE = 640
HALF = ROPE // 2

rope_base = 50000.0
masked_value = -1e30
softmax_scale = float(NOPE + ROPE) ** (-0.5)
log2_scale = softmax_scale * 1.4426950408889634

MIB = 1 << 20
bf16 = jnp.bfloat16
f32 = jnp.float32


def vmem():
    return pl.BlockSpec(memory_space=pltpu.VMEM)


def hbm():
    return pl.BlockSpec(memory_space=pltpu.HBM)


def anywhere():
    return pl.BlockSpec(memory_space=pl.ANY)


def smem():
    return pl.BlockSpec(memory_space=pltpu.SMEM)


def select_kernel(table_ref, pool_ref, out_ref, pos_ref):
    group = lax.axis_index("group")
    page_rows, _, slot_count = pool_ref.shape
    requests, max_pages = table_ref.shape
    shift = slot_count.bit_length() - 1
    rows = requests * CAP * page_rows
    table = table_ref[...]
    page = lax.broadcasted_iota(jnp.int32, table.shape, 1)
    code = page * slot_count + (table & (slot_count - 1))
    mine = (table >> shift) == group
    first = jnp.min(jnp.where(mine, code, max_pages * slot_count), axis=1, keepdims=True) & (slot_count - 1)
    last = jnp.max(jnp.where(mine, code, 0), axis=1, keepdims=True) & (slot_count - 1)
    shape = (requests, CAP * page_rows, slot_count)
    part = lax.broadcasted_iota(jnp.int32, shape, 1)
    slot = lax.broadcasted_iota(jnp.int32, shape, 2)
    first = jnp.broadcast_to(first[:, :, None], shape)
    last = jnp.broadcast_to(last[:, :, None], shape)
    hit = slot == jnp.where(part < page_rows, first, last)
    total = None
    for u in range(page_rows):
        pick = jnp.where(jnp.logical_and(hit, part % page_rows == u), 1.0, 0.0).reshape(rows, slot_count).astype(bf16)
        term = lax.dot_general(pick, pool_ref[u], (((1,), (1,)), ((), ())), preferred_element_type=f32)
        total = term if total is None else total + term
    out_ref[...] = total.astype(bf16)
    owners = table_ref[pl.ds(group, 1), :] >> shift
    row = lax.broadcasted_iota(jnp.int32, (rows, max_pages), 0)
    column = lax.broadcasted_iota(jnp.int32, (rows, max_pages), 1)
    held = owners == row // (CAP * page_rows)
    first_page = jnp.min(jnp.where(held, column, max_pages), axis=1, keepdims=True)
    last_page = jnp.max(jnp.where(held, column, 0), axis=1, keepdims=True)
    one_row = lax.broadcasted_iota(jnp.int32, (rows, 1), 0)
    at = jnp.where((one_row // page_rows) % CAP == 0, first_page, last_page)
    pos_ref[...] = at * (page_rows * 8) + one_row % page_rows


def select(page_table, pool):
    rows = page_table.shape[0] * CAP * pool.shape[1]
    return pl.pallas_call(
        select_kernel,
        in_specs=[vmem(), vmem()],
        out_specs=[vmem(), vmem()],
        out_shape=[jax.ShapeDtypeStruct((rows, LAT), bf16), jax.ShapeDtypeStruct((rows, 1), jnp.int32)],
        compiler_params=pltpu.CompilerParams(vmem_limit_bytes=59 * MIB),
        cost_estimate=pl.CostEstimate(flops=8 * rows * 128 * LAT, bytes_accessed=1000000, transcendentals=0),
        name="select",
    )(page_table, jnp.transpose(pool, (1, 2, 0)))


def project_kernel(x_ref, w_ref, out_ref):
    total = lax.dot_general(x_ref[...], w_ref[...], (((1,), (1,)), ((), ())), preferred_element_type=f32)
    out_ref[...] = total.astype(bf16)


def project(x, w):
    return pl.pallas_call(
        project_kernel,
        in_specs=[vmem(), vmem()],
        out_specs=vmem(),
        out_shape=jax.ShapeDtypeStruct((x.shape[0], w.shape[0]), bf16),
        compiler_params=pltpu.CompilerParams(vmem_limit_bytes=8 * MIB),
        cost_estimate=pl.CostEstimate(flops=2 * x.size * w.shape[0], bytes_accessed=2 * (x.size + w.size),
                                      transcendentals=0),
        name="project",
    )(x, w)


def rotary(frequency, length, first_token, tokens):
    token = first_token + lax.broadcasted_iota(jnp.int32, (HALF, tokens), 1)
    angles = frequency * (length + token).astype(f32)
    return jnp.cos(angles), jnp.sin(angles)


def query_kernel(length_ref, frequency_ref, ql_ref, wq_hbm, out_ref, done_ref, wq_ref, sems):
    done_ref[...] = jnp.zeros_like(done_ref)
    heads, _, tokens = out_ref.shape
    pair_width = 2 * (NOPE + ROPE)
    copies = []
    for pair in range(heads // 2):
        columns = pl.ds(pair * pair_width, pair_width)
        copy = pltpu.make_async_copy(wq_hbm.at[:, columns], wq_ref.at[pair], sems.at[pair])
        copy.start()
        copies.append(copy)
    cosine, sine = rotary(frequency_ref[...], length_ref[lax.axis_index("group")], 0, tokens)
    row = lax.broadcasted_iota(jnp.int32, (QWIDE - NOPE - ROPE, tokens), 0)
    tail = jnp.where(row == 0, 1.0, 0.0).astype(bf16)
    for pair in range(heads // 2):
        copies[pair].wait()
        qt = jnp.dot(ql_ref[...], wq_ref[pair], preferred_element_type=f32).T
        for i in range(2):
            h = 2 * pair + i
            base = i * (NOPE + ROPE)
            first = qt[base + NOPE:base + NOPE + HALF]
            second = qt[base + NOPE + HALF:base + NOPE + ROPE]
            out_ref[h, :NOPE, :] = qt[base:base + NOPE].astype(bf16)
            out_ref[h, NOPE:NOPE + HALF, :] = (first * cosine - second * sine).astype(bf16)
            out_ref[h, NOPE + HALF:NOPE + ROPE, :] = (second * cosine + first * sine).astype(bf16)
            out_ref[h, NOPE + ROPE:, :] = tail


def make_queries(prefix_len, frequency, q_latent, w_q_b):
    tokens, rank = q_latent.shape
    heads = w_q_b.shape[1] // (NOPE + ROPE)
    return pl.pallas_call(
        query_kernel,
        in_specs=[smem(), vmem(), vmem(), hbm()],
        out_specs=[vmem(), vmem()],
        out_shape=[
            jax.ShapeDtypeStruct((heads, QWIDE, tokens), bf16),
            jax.ShapeDtypeStruct((8, 128), f32),
        ],
        scratch_shapes=[
            pltpu.VMEM((heads // 2, rank, 2 * (NOPE + ROPE)), bf16),
            pltpu.SemaphoreType.DMA((heads // 2,)),
        ],
        compiler_params=pltpu.CompilerParams(vmem_limit_bytes=56 * MIB),
        cost_estimate=pl.CostEstimate(flops=2 * tokens * rank * heads * 192, bytes_accessed=6 * MIB, transcendentals=0),
        name="queries",
    )(prefix_len, frequency, q_latent, w_q_b)


def combine_kernel(a_ref, b_ref, own_ref, up_ref, down_ref, far_ref):
    y = lax.axis_index("tensor") // 2
    rows = own_ref.shape[0]

    def part(d):
        start = pl.multiple_of(lax.rem(y + d, 4) * rows, rows)
        return a_ref[pl.ds(start, rows), :].astype(f32) + b_ref[pl.ds(start, rows), :].astype(f32)

    own_ref[...] = part(0)
    up_ref[...] = part(1).astype(bf16)
    far_ref[...] = part(2).astype(bf16)
    down_ref[...] = part(3).astype(bf16)


def combine(a, b):
    rows = a.shape[0] // 4
    return pl.pallas_call(
        combine_kernel,
        in_specs=[vmem(), vmem()],
        out_specs=[vmem()] * 4,
        out_shape=[jax.ShapeDtypeStruct((rows, LAT), f32)] + [jax.ShapeDtypeStruct((rows, LAT), bf16)] * 3,
        compiler_params=pltpu.CompilerParams(vmem_limit_bytes=4 * MIB),
        cost_estimate=pl.CostEstimate(flops=a.size, bytes_accessed=8 * a.size, transcendentals=0),
        name="combine",
    )(a, b)


def finish_kernel(length_ref, frequency_ref, own_ref, a_ref, b_ref, c_ref, gain_ref, out_ref, share_ref):
    total = (own_ref[...] + a_ref[...].astype(f32)) + (b_ref[...].astype(f32) + c_ref[...].astype(f32))
    rows = total.shape[0]
    nope = total[:, :KVR]
    mean_square = jnp.mean(nope * nope, axis=-1, keepdims=True)
    turned = total[:, KVR:LAT].T
    first = turned[:HALF]
    second = turned[HALF:]
    tensor = lax.axis_index("tensor")
    length = length_ref[lax.axis_index("group")]
    cosine, sine = rotary(frequency_ref[...], length, tensor // 2 * rows, rows)
    rotated = jnp.concatenate([first * cosine - second * sine, second * cosine + first * sine], axis=0).T
    out_ref[:, :KVR] = (nope * lax.rsqrt(mean_square + 1e-06) * gain_ref[...]).astype(bf16)
    out_ref[:, KVR:LAT] = rotated.astype(bf16)
    half = rows // 2
    core = lax.rem(tensor, 2)
    share_ref[...] = out_ref[pl.ds(pl.multiple_of(core * half, half), half), :]


def finish(prefix_len, frequency, own, a, b, c, gain):
    rows = own.shape[0]
    return pl.pallas_call(
        finish_kernel,
        in_specs=[smem()] + [vmem()] * 6,
        out_specs=[vmem(), vmem()],
        out_shape=[jax.ShapeDtypeStruct(own.shape, bf16), jax.ShapeDtypeStruct((rows // 2, LAT), bf16)],
        compiler_params=pltpu.CompilerParams(vmem_limit_bytes=4 * MIB),
        cost_estimate=pl.CostEstimate(flops=8 * own.size, bytes_accessed=12 * own.size, transcendentals=0),
        name="finish",
    )(prefix_len, frequency, own, a, b, c, gain)


def address_kernel(owner_ref, *refs):
    in_refs, out_ref = refs[:4], refs[4]
    group = lax.axis_index("group")
    x = lax.rem(group, 4)
    out_ref[...] = jnp.zeros_like(out_ref)
    for turn in range(4):
        owner = owner_ref[group - x + lax.rem(x - turn + 4, 4)]

        @pl.when(lax.rem(owner, 4) == x)
        def _():
            out_ref[owner // 4] = in_refs[turn][...]


def address(decode_owner, shares):
    rows = shares[0].shape[0]
    return pl.pallas_call(
        address_kernel,
        in_specs=[smem()] + [vmem()] * 4,
        out_specs=vmem(),
        out_shape=jax.ShapeDtypeStruct((8, rows, LAT), bf16),
        compiler_params=pltpu.CompilerParams(vmem_limit_bytes=4 * MIB),
        cost_estimate=pl.CostEstimate(flops=1000, bytes_accessed=20 * rows * LAT, transcendentals=0),
        name="address",
    )(decode_owner, *shares)


def pick_kernel(owner_ref, in_ref, _, out_ref, sem):
    group = lax.axis_index("group")
    request = jnp.int32(0)
    for r in range(owner_ref.shape[0]):
        request = request + jnp.where(owner_ref[r] == group, r, 0)
    copy = pltpu.make_async_copy(in_ref.at[request // 4], out_ref, sem)
    copy.start()
    copy.wait()


def pick(decode_owner, arrived, earlier):
    rows = arrived.shape[1]
    return pl.pallas_call(
        pick_kernel,
        in_specs=[smem(), anywhere(), anywhere()],
        out_specs=vmem(),
        out_shape=jax.ShapeDtypeStruct((rows, LAT), bf16),
        scratch_shapes=[pltpu.SemaphoreType.DMA],
        compiler_params=pltpu.CompilerParams(vmem_limit_bytes=4 * MIB),
        cost_estimate=pl.CostEstimate(flops=1000, bytes_accessed=4 * rows * LAT, transcendentals=0),
        name="pick",
    )(decode_owner, arrived, earlier)


def copies_kernel(x_ref, _, __, out_ref):
    x = x_ref[...]
    for i in range(out_ref.shape[0]):
        out_ref[i, :, :LAT] = x
        out_ref[i, :, LAT:] = jnp.zeros((x.shape[0], WIDE - LAT), bf16)


def four_copies(x, *tokens):
    return pl.pallas_call(
        copies_kernel,
        in_specs=[vmem(), anywhere(), anywhere()],
        out_specs=vmem(),
        out_shape=jax.ShapeDtypeStruct((4, x.shape[0], WIDE), x.dtype),
        compiler_params=pltpu.CompilerParams(vmem_limit_bytes=8 * MIB),
        cost_estimate=pl.CostEstimate(flops=0, bytes_accessed=10 * x.size, transcendentals=0),
        name="four_copies",
    )(x, *tokens)


def again_kernel(x_ref, *refs):
    out_ref, sems = refs[-2:]
    copies = [pltpu.make_async_copy(x_ref.at[i], out_ref.at[i], sems.at[i]) for i in range(out_ref.shape[0])]
    for copy in copies:
        copy.start()
    for copy in copies:
        copy.wait()


def again(x, *tokens):
    return pl.pallas_call(
        again_kernel,
        in_specs=[anywhere()] * (1 + len(tokens)),
        out_specs=hbm(),
        out_shape=jax.ShapeDtypeStruct(x.shape, x.dtype),
        scratch_shapes=[pltpu.SemaphoreType.DMA((x.shape[0],))],
        compiler_params=pltpu.CompilerParams(vmem_limit_bytes=4 * MIB),
        cost_estimate=pl.CostEstimate(flops=0, bytes_accessed=4 * x.size, transcendentals=0),
        name="again",
    )(x, *tokens)


def attention_kernel(turns, length_ref, pos_ref, qt_ref, wk_hbm, wv_hbm, same_ref, other_ref, *refs):
    refs = list(refs)
    new_refs = [refs.pop(0) for _ in turns]
    out_ref, tails, keys, values, scores, weights, landed, fresh, turned, wk_ref, wv_ref, wv_turned, sems, w_sems = refs
    heads, _, tokens = qt_ref.shape
    rows = pos_ref.shape[0]
    blocks = 8
    tiles = blocks + 1
    tensor = lax.axis_index("tensor")
    length = length_ref[lax.axis_index("group")]
    core = lax.rem(tensor, 2)
    ups = []
    for pair in range(heads // 2):
        columns = pl.ds(pair * 256, 256)
        for i, (source, target) in enumerate(((wk_hbm, wk_ref), (wv_hbm, wv_ref))):
            ups.append(pltpu.make_async_copy(source.at[:, columns], target.at[:, columns], w_sems.at[2 * pair + i]))
    copies = []
    for b in range(blocks):
        copies.append(pltpu.make_async_copy((same_ref if b < 4 else other_ref).at[b % 4], landed.at[b], sems.at[b]))
    for copy in ups[:2] + copies:
        copy.start()
    latents = [landed.at[b] for b in range(blocks)] + [fresh]
    causal = []
    for b, turn in enumerate(turns):
        n = new_refs[b].shape[0]
        fresh[b * n:(b + 1) * n, :] = new_refs[b][...]
        key_token = lax.rem(tensor // 2 + turn, 4) * n + lax.broadcasted_iota(jnp.int32, (n, tokens), 0)
        causal.append(key_token <= lax.broadcasted_iota(jnp.int32, (n, tokens), 1))
    allowed = jnp.concatenate(causal, axis=0)
    lane = lax.broadcasted_iota(jnp.int32, (rows, 128 - ROPE), 1)

    def stage(j):
        here = slice(j * rows, (j + 1) * rows)
        if j < blocks:
            copies[j].wait()
            source = 2 * (j % 4) + (core if j < 4 else 1 - core)
            out_of_range = jnp.logical_and(pos_ref[...] >= length - 4 * source, lane == 0)
            tails[here, ROPE:] = jnp.where(out_of_range, masked_value, 0.0).astype(bf16)
        else:
            tails[here, ROPE:] = jnp.zeros((rows, 128 - ROPE), bf16)
        tails[here, :ROPE] = latents[j][:, KVR:LAT]
        turned[:, here] = latents[j][:, :KVR].T

    def await_weights(pair):
        columns = slice(pair * 256, (pair + 1) * 256)
        for copy in ups[2 * pair:2 * pair + 2]:
            copy.wait()
        wv_turned[columns, :] = wv_ref[:, columns].T

    def project_up(pair, j):
        here = slice(j * rows, (j + 1) * rows)
        nope = latents[j][:, :KVR]
        columns = slice(pair * 256, (pair + 1) * 256)
        k = jnp.dot(nope, wk_ref[:, columns], preferred_element_type=f32).astype(bf16)
        v = jnp.dot(wv_turned[columns, :], turned[:, here], preferred_element_type=f32).astype(bf16)
        for i in range(2):
            slot = 2 * (pair % 2) + i
            keys[slot, here, :NOPE] = k[:, i * NOPE:(i + 1) * NOPE]
            keys[slot, here, NOPE:] = tails[here, :]
            values[2 * (pair % 3) + i, :, here] = v[i * VDIM:(i + 1) * VDIM]

    def score(h, j):
        here = slice(j * rows, (j + 1) * rows)
        s = jnp.dot(keys[h % 4, here], qt_ref[h], preferred_element_type=f32)
        if j >= blocks:
            s = jnp.where(allowed, s, masked_value)
        scores[h % 2, here] = s
        return jnp.max(s, axis=0, keepdims=True)

    def weigh(h, j, top):
        here = slice(j * rows, (j + 1) * rows)
        p = jnp.exp2((scores[h % 2, here] - top) * log2_scale)
        weights[h % 2, here] = p.astype(bf16)
        return jnp.sum(p, axis=0, keepdims=True)

    def gather_values(h, norm):
        acc = jnp.dot(values[2 * (h // 2 % 3) + h % 2], weights[h % 2], preferred_element_type=f32)
        out_ref[:, h * VDIM:(h + 1) * VDIM] = (acc / norm).T.astype(bf16)

    order = [blocks] + list(range(blocks))
    tops = []
    await_weights(0)
    for i, j in enumerate(order):
        stage(j)
        if i == 3:
            for copy in ups[2:]:
                copy.start()
        project_up(0, j)
        tops.append(score(0, j))
    for h in range(heads):
        top = functools.reduce(jnp.maximum, tops)
        tops = []
        norms = []
        if h % 2 == 0 and h + 2 < heads:
            await_weights(h // 2 + 1)
        for i, j in enumerate(order):
            if h // 2 * 2 + 2 < heads and i % 2 == h % 2:
                project_up(h // 2 + 1, j)
            if h + 1 < heads:
                tops.append(score(h + 1, j))
            norms.append(weigh(h, j, top))
            if i == 2 and h > 0:
                gather_values(h - 1, norm)
        norm = functools.reduce(jnp.add, norms)
    gather_values(heads - 1, norm)


def attention(prefix_len, pos, qt, w_key_up, w_value_up, cached, turns, new_blocks):
    heads, _, tokens = qt.shape
    rows = pos.shape[0]
    blocks = 8
    total = rows * (blocks + 1)
    return pl.pallas_call(
        functools.partial(attention_kernel, turns),
        in_specs=[smem()] + [vmem()] * 2 + [hbm()] * 4 + [vmem()] * len(new_blocks),
        out_specs=vmem(),
        out_shape=jax.ShapeDtypeStruct((tokens, heads * VDIM), bf16),
        scratch_shapes=[
            pltpu.VMEM((total, 128), bf16),
            pltpu.VMEM((4, total, QWIDE), bf16),
            pltpu.VMEM((6, VDIM, total), bf16),
            pltpu.VMEM((2, total, tokens), f32),
            pltpu.VMEM((2, total, tokens), bf16),
            pltpu.VMEM((blocks, rows, WIDE), bf16),
            pltpu.VMEM((rows, LAT), bf16),
            pltpu.VMEM((KVR, total), bf16),
            pltpu.VMEM(w_key_up.shape, bf16),
            pltpu.VMEM(w_value_up.shape, bf16),
            pltpu.VMEM(w_value_up.shape[::-1], bf16),
            pltpu.SemaphoreType.DMA((blocks,)),
            pltpu.SemaphoreType.DMA((heads,)),
        ],
        compiler_params=pltpu.CompilerParams(vmem_limit_bytes=58 * MIB),
        cost_estimate=pl.CostEstimate(flops=4 * heads * tokens * total * 512, bytes_accessed=4 * MIB,
                                      transcendentals=heads * tokens * total),
        name="attention",
    )(prefix_len, pos, qt, w_key_up, w_value_up, *cached, *new_blocks)


def shards(
    hidden,
    w_kv_a,
    kv_gain,
    q_latent,
    w_q_b,
    w_key_up,
    w_value_up,
    pool,
    page_table,
    prefix_len,
    decode_owner,
):

    def tensor_permute(x, step):
        return lax.ppermute(x, "tensor", [(i, step(i)) for i in range(8)])

    up = lambda i: (i + 2) % 8
    down = lambda i: (i - 2) % 8
    far = lambda i: (i + 4) % 8
    other = lambda i: i ^ 1

    outgoing, pos = select(page_table, pool)
    outgoing = outgoing.reshape(page_table.shape[0], -1, LAT)
    incoming = lax.all_to_all(outgoing, "group", split_axis=0, concat_axis=0, tiled=True)
    own_block = incoming.reshape(pos.shape[0], LAT)

    frequency = jnp.asarray((rope_base ** (-2.0 * np.arange(HALF) / ROPE)).astype(np.float32)[:, None])

    qt, queried = make_queries(prefix_len, frequency, q_latent, w_q_b)

    partial_sum = project(hidden, w_kv_a.T)
    partner_sum = tensor_permute(partial_sum, other)
    own, to_up, to_down, to_far = combine(partial_sum, partner_sum)
    from_down = tensor_permute(to_up, up)
    from_up = tensor_permute(to_down, down)
    from_far = tensor_permute(to_far, far)
    latent, share = finish(prefix_len, frequency, own, from_down, from_up, from_far, kv_gain[None, :])
    latents = [latent, tensor_permute(latent, up), tensor_permute(latent, down), tensor_permute(latent, far)]

    def x_permute(turn):
        return lax.ppermute(share, "group", [(i, i // 4 * 4 + (i + turn) % 4) for i in range(32)])

    columns = [[4 * z + x for z in range(8)] for x in range(4)]
    addressed = address(decode_owner, [share, x_permute(1), x_permute(2), x_permute(3)])
    arrived = lax.all_to_all(addressed, "group", 0, 0, tiled=True, axis_index_groups=columns)

    same_core = lax.all_to_all(
        four_copies(own_block, latent, queried), "tensor", 0, 0, tiled=True, axis_index_groups=[[0, 2, 4, 6], [1, 3, 5, 7]]
    )
    same_core = again(same_core, addressed, *latents[1:])
    cached = [same_core, tensor_permute(same_core, other)]
    attn_out = attention(prefix_len, pos, qt, w_key_up, w_value_up, cached, (0, 3, 1, 2), latents)
    decode_pages = pick(decode_owner, arrived, attn_out)
    return (attn_out, decode_pages)


def solution(mesh):
    return jax.shard_map(
        shards,
        mesh=mesh,
        in_specs=(
            P("group", "tensor"),
            P("tensor", None),
            P(),
            P("group", None),
            P(None, "tensor"),
            P(None, "tensor"),
            P(None, "tensor"),
            P("group", "tensor", None),
            P(),
            P(),
            P(),
        ),
        out_specs=(P("group", "tensor"), P(("group", "tensor"), None)),
        check_vma=False,
    )
```

```python
import functools

import jax
import jax.numpy as jnp
import numpy as np
from jax import lax
from jax.experimental import pallas as pl
from jax.experimental.pallas import tpu as pltpu
from jax.sharding import PartitionSpec as P

NOPE = 128
ROPE = 64
VDIM = 128
KVR = 512
CAP = 2
LAT = KVR + ROPE
QWIDE = 256
WIDE = 640
HALF = ROPE // 2

rope_base = 50000.0
masked_value = -1e30
softmax_scale = float(NOPE + ROPE) ** (-0.5)
log2_scale = softmax_scale * 1.4426950408889634

MIB = 1 << 20
bf16 = jnp.bfloat16
f32 = jnp.float32


def vmem():
    return pl.BlockSpec(memory_space=pltpu.VMEM)


def hbm():
    return pl.BlockSpec(memory_space=pltpu.HBM)


def anywhere():
    return pl.BlockSpec(memory_space=pl.ANY)


def smem():
    return pl.BlockSpec(memory_space=pltpu.SMEM)


def select_kernel(table_ref, pool_ref, out_ref, pos_ref):
    group = lax.axis_index("group")
    page_rows, _, slot_count = pool_ref.shape
    requests, max_pages = table_ref.shape
    shift = slot_count.bit_length() - 1
    rows = requests * CAP * page_rows
    table = table_ref[...]
    page = lax.broadcasted_iota(jnp.int32, table.shape, 1)
    code = page * slot_count + (table & (slot_count - 1))
    mine = (table >> shift) == group
    first = jnp.min(jnp.where(mine, code, max_pages * slot_count), axis=1, keepdims=True) & (slot_count - 1)
    last = jnp.max(jnp.where(mine, code, 0), axis=1, keepdims=True) & (slot_count - 1)
    shape = (requests, CAP * page_rows, slot_count)
    part = lax.broadcasted_iota(jnp.int32, shape, 1)
    slot = lax.broadcasted_iota(jnp.int32, shape, 2)
    first = jnp.broadcast_to(first[:, :, None], shape)
    last = jnp.broadcast_to(last[:, :, None], shape)
    hit = slot == jnp.where(part < page_rows, first, last)
    total = None
    for u in range(page_rows):
        pick = jnp.where(jnp.logical_and(hit, part % page_rows == u), 1.0, 0.0).reshape(rows, slot_count).astype(bf16)
        term = lax.dot_general(pick, pool_ref[u], (((1,), (1,)), ((), ())), preferred_element_type=f32)
        total = term if total is None else total + term
    out_ref[...] = total.astype(bf16)
    owners = table_ref[pl.ds(group, 1), :] >> shift
    row = lax.broadcasted_iota(jnp.int32, (rows, max_pages), 0)
    column = lax.broadcasted_iota(jnp.int32, (rows, max_pages), 1)
    held = owners == row // (CAP * page_rows)
    first_page = jnp.min(jnp.where(held, column, max_pages), axis=1, keepdims=True)
    last_page = jnp.max(jnp.where(held, column, 0), axis=1, keepdims=True)
    one_row = lax.broadcasted_iota(jnp.int32, (rows, 1), 0)
    at = jnp.where((one_row // page_rows) % CAP == 0, first_page, last_page)
    pos_ref[...] = at * (page_rows * 8) + one_row % page_rows


def select(page_table, pool):
    rows = page_table.shape[0] * CAP * pool.shape[1]
    return pl.pallas_call(
        select_kernel,
        in_specs=[vmem(), vmem()],
        out_specs=[vmem(), vmem()],
        out_shape=[jax.ShapeDtypeStruct((rows, LAT), bf16), jax.ShapeDtypeStruct((rows, 1), jnp.int32)],
        compiler_params=pltpu.CompilerParams(vmem_limit_bytes=59 * MIB),
        cost_estimate=pl.CostEstimate(flops=8 * rows * 128 * LAT, bytes_accessed=1000000, transcendentals=0),
        name="select",
    )(page_table, jnp.transpose(pool, (1, 2, 0)))


def project_kernel(x_ref, w_ref, out_ref):
    total = lax.dot_general(x_ref[...], w_ref[...], (((1,), (1,)), ((), ())), preferred_element_type=f32)
    out_ref[...] = total.astype(bf16)


def project(x, w):
    return pl.pallas_call(
        project_kernel,
        in_specs=[vmem(), vmem()],
        out_specs=vmem(),
        out_shape=jax.ShapeDtypeStruct((x.shape[0], w.shape[0]), bf16),
        compiler_params=pltpu.CompilerParams(vmem_limit_bytes=8 * MIB),
        cost_estimate=pl.CostEstimate(flops=2 * x.size * w.shape[0], bytes_accessed=2 * (x.size + w.size),
                                      transcendentals=0),
        name="project",
    )(x, w)


def rotary(frequency, length, first_token, tokens):
    token = first_token + lax.broadcasted_iota(jnp.int32, (HALF, tokens), 1)
    angles = frequency * (length + token).astype(f32)
    return jnp.cos(angles), jnp.sin(angles)


def query_kernel(length_ref, frequency_ref, ql_ref, wq_hbm, out_ref, done_ref, wq_ref, sems):
    done_ref[...] = jnp.zeros_like(done_ref)
    heads, _, tokens = out_ref.shape
    pair_width = 2 * (NOPE + ROPE)
    copies = []
    for pair in range(heads // 2):
        columns = pl.ds(pair * pair_width, pair_width)
        copy = pltpu.make_async_copy(wq_hbm.at[:, columns], wq_ref.at[pair], sems.at[pair])
        copy.start()
        copies.append(copy)
    cosine, sine = rotary(frequency_ref[...], length_ref[lax.axis_index("group")], 0, tokens)
    row = lax.broadcasted_iota(jnp.int32, (QWIDE - NOPE - ROPE, tokens), 0)
    tail = jnp.where(row == 0, 1.0, 0.0).astype(bf16)
    for pair in range(heads // 2):
        copies[pair].wait()
        qt = jnp.dot(ql_ref[...], wq_ref[pair], preferred_element_type=f32).T
        for i in range(2):
            h = 2 * pair + i
            base = i * (NOPE + ROPE)
            first = qt[base + NOPE:base + NOPE + HALF]
            second = qt[base + NOPE + HALF:base + NOPE + ROPE]
            out_ref[h, :NOPE, :] = qt[base:base + NOPE].astype(bf16)
            out_ref[h, NOPE:NOPE + HALF, :] = (first * cosine - second * sine).astype(bf16)
            out_ref[h, NOPE + HALF:NOPE + ROPE, :] = (second * cosine + first * sine).astype(bf16)
            out_ref[h, NOPE + ROPE:, :] = tail


def make_queries(prefix_len, frequency, q_latent, w_q_b):
    tokens, rank = q_latent.shape
    heads = w_q_b.shape[1] // (NOPE + ROPE)
    return pl.pallas_call(
        query_kernel,
        in_specs=[smem(), vmem(), vmem(), hbm()],
        out_specs=[vmem(), vmem()],
        out_shape=[
            jax.ShapeDtypeStruct((heads, QWIDE, tokens), bf16),
            jax.ShapeDtypeStruct((8, 128), f32),
        ],
        scratch_shapes=[
            pltpu.VMEM((heads // 2, rank, 2 * (NOPE + ROPE)), bf16),
            pltpu.SemaphoreType.DMA((heads // 2,)),
        ],
        compiler_params=pltpu.CompilerParams(vmem_limit_bytes=56 * MIB),
        cost_estimate=pl.CostEstimate(flops=2 * tokens * rank * heads * 192, bytes_accessed=6 * MIB, transcendentals=0),
        name="queries",
    )(prefix_len, frequency, q_latent, w_q_b)


def combine_kernel(a_ref, b_ref, own_ref, up_ref, down_ref, far_ref):
    y = lax.axis_index("tensor") // 2
    rows = own_ref.shape[0]

    def part(d):
        start = pl.multiple_of(lax.rem(y + d, 4) * rows, rows)
        return a_ref[pl.ds(start, rows), :].astype(f32) + b_ref[pl.ds(start, rows), :].astype(f32)

    own_ref[...] = part(0)
    up_ref[...] = part(1).astype(bf16)
    far_ref[...] = part(2).astype(bf16)
    down_ref[...] = part(3).astype(bf16)


def combine(a, b):
    rows = a.shape[0] // 4
    return pl.pallas_call(
        combine_kernel,
        in_specs=[vmem(), vmem()],
        out_specs=[vmem()] * 4,
        out_shape=[jax.ShapeDtypeStruct((rows, LAT), f32)] + [jax.ShapeDtypeStruct((rows, LAT), bf16)] * 3,
        compiler_params=pltpu.CompilerParams(vmem_limit_bytes=4 * MIB),
        cost_estimate=pl.CostEstimate(flops=a.size, bytes_accessed=8 * a.size, transcendentals=0),
        name="combine",
    )(a, b)


def finish_kernel(length_ref, frequency_ref, own_ref, a_ref, b_ref, c_ref, gain_ref, out_ref, share_ref):
    total = (own_ref[...] + a_ref[...].astype(f32)) + (b_ref[...].astype(f32) + c_ref[...].astype(f32))
    rows = total.shape[0]
    nope = total[:, :KVR]
    mean_square = jnp.mean(nope * nope, axis=-1, keepdims=True)
    turned = total[:, KVR:LAT].T
    first = turned[:HALF]
    second = turned[HALF:]
    tensor = lax.axis_index("tensor")
    length = length_ref[lax.axis_index("group")]
    cosine, sine = rotary(frequency_ref[...], length, tensor // 2 * rows, rows)
    rotated = jnp.concatenate([first * cosine - second * sine, second * cosine + first * sine], axis=0).T
    out_ref[:, :KVR] = (nope * lax.rsqrt(mean_square + 1e-06) * gain_ref[...]).astype(bf16)
    out_ref[:, KVR:LAT] = rotated.astype(bf16)
    half = rows // 2
    core = lax.rem(tensor, 2)
    share_ref[...] = out_ref[pl.ds(pl.multiple_of(core * half, half), half), :]


def finish(prefix_len, frequency, own, a, b, c, gain):
    rows = own.shape[0]
    return pl.pallas_call(
        finish_kernel,
        in_specs=[smem()] + [vmem()] * 6,
        out_specs=[vmem(), vmem()],
        out_shape=[jax.ShapeDtypeStruct(own.shape, bf16), jax.ShapeDtypeStruct((rows // 2, LAT), bf16)],
        compiler_params=pltpu.CompilerParams(vmem_limit_bytes=4 * MIB),
        cost_estimate=pl.CostEstimate(flops=8 * own.size, bytes_accessed=12 * own.size, transcendentals=0),
        name="finish",
    )(prefix_len, frequency, own, a, b, c, gain)


def address_kernel(owner_ref, *refs):
    in_refs, out_ref = refs[:4], refs[4]
    group = lax.axis_index("group")
    x = lax.rem(group, 4)
    out_ref[...] = jnp.zeros_like(out_ref)
    for turn in range(4):
        owner = owner_ref[group - x + lax.rem(x - turn + 4, 4)]

        @pl.when(lax.rem(owner, 4) == x)
        def _():
            out_ref[owner // 4] = in_refs[turn][...]


def address(decode_owner, shares):
    rows = shares[0].shape[0]
    return pl.pallas_call(
        address_kernel,
        in_specs=[smem()] + [vmem()] * 4,
        out_specs=vmem(),
        out_shape=jax.ShapeDtypeStruct((8, rows, LAT), bf16),
        compiler_params=pltpu.CompilerParams(vmem_limit_bytes=4 * MIB),
        cost_estimate=pl.CostEstimate(flops=1000, bytes_accessed=20 * rows * LAT, transcendentals=0),
        name="address",
    )(decode_owner, *shares)


def pick_kernel(owner_ref, in_ref, _, out_ref, sem):
    group = lax.axis_index("group")
    request = jnp.int32(0)
    for r in range(owner_ref.shape[0]):
        request = request + jnp.where(owner_ref[r] == group, r, 0)
    copy = pltpu.make_async_copy(in_ref.at[request // 4], out_ref, sem)
    copy.start()
    copy.wait()


def pick(decode_owner, arrived, earlier):
    rows = arrived.shape[1]
    return pl.pallas_call(
        pick_kernel,
        in_specs=[smem(), anywhere(), anywhere()],
        out_specs=vmem(),
        out_shape=jax.ShapeDtypeStruct((rows, LAT), bf16),
        scratch_shapes=[pltpu.SemaphoreType.DMA],
        compiler_params=pltpu.CompilerParams(vmem_limit_bytes=4 * MIB),
        cost_estimate=pl.CostEstimate(flops=1000, bytes_accessed=4 * rows * LAT, transcendentals=0),
        name="pick",
    )(decode_owner, arrived, earlier)


def copies_kernel(x_ref, _, __, out_ref):
    x = x_ref[...]
    for i in range(out_ref.shape[0]):
        out_ref[i, :, :LAT] = x
        out_ref[i, :, LAT:] = jnp.zeros((x.shape[0], WIDE - LAT), bf16)


def four_copies(x, *tokens):
    return pl.pallas_call(
        copies_kernel,
        in_specs=[vmem(), anywhere(), anywhere()],
        out_specs=vmem(),
        out_shape=jax.ShapeDtypeStruct((4, x.shape[0], WIDE), x.dtype),
        compiler_params=pltpu.CompilerParams(vmem_limit_bytes=8 * MIB),
        cost_estimate=pl.CostEstimate(flops=0, bytes_accessed=10 * x.size, transcendentals=0),
        name="four_copies",
    )(x, *tokens)


def again_kernel(x_ref, *refs):
    out_ref, sems = refs[-2:]
    copies = [pltpu.make_async_copy(x_ref.at[i], out_ref.at[i], sems.at[i]) for i in range(out_ref.shape[0])]
    for copy in copies:
        copy.start()
    for copy in copies:
        copy.wait()


def again(x, *tokens):
    return pl.pallas_call(
        again_kernel,
        in_specs=[anywhere()] * (1 + len(tokens)),
        out_specs=hbm(),
        out_shape=jax.ShapeDtypeStruct(x.shape, x.dtype),
        scratch_shapes=[pltpu.SemaphoreType.DMA((x.shape[0],))],
        compiler_params=pltpu.CompilerParams(vmem_limit_bytes=4 * MIB),
        cost_estimate=pl.CostEstimate(flops=0, bytes_accessed=4 * x.size, transcendentals=0),
        name="again",
    )(x, *tokens)


def attention_kernel(turns, length_ref, pos_ref, qt_ref, wk_hbm, wv_hbm, same_ref, other_ref, *refs):
    refs = list(refs)
    new_refs = [refs.pop(0) for _ in turns]
    out_ref, done_ref, tails, keys, values, scores, weights, fresh, turned, wk_ref, wv_ref, wv_turned, w_sems = refs
    done_ref[...] = jnp.zeros_like(done_ref)
    heads, _, tokens = qt_ref.shape
    rows = pos_ref.shape[0]
    blocks = 8
    tiles = blocks + 1
    tensor = lax.axis_index("tensor")
    length = length_ref[lax.axis_index("group")]
    core = lax.rem(tensor, 2)
    ups = []
    for pair in range(heads // 2):
        columns = pl.ds(pair * 256, 256)
        for i, (source, target) in enumerate(((wk_hbm, wk_ref), (wv_hbm, wv_ref))):
            ups.append(pltpu.make_async_copy(source.at[:, columns], target.at[:, columns], w_sems.at[2 * pair + i]))
    for copy in ups:
        copy.start()
    latents = [ref.at[y] for ref in (same_ref, other_ref) for y in range(4)] + [fresh]
    causal = []
    for b, turn in enumerate(turns):
        n = new_refs[b].shape[0]
        fresh[b * n:(b + 1) * n, :] = new_refs[b][...]
        key_token = lax.rem(tensor // 2 + turn, 4) * n + lax.broadcasted_iota(jnp.int32, (n, tokens), 0)
        causal.append(key_token <= lax.broadcasted_iota(jnp.int32, (n, tokens), 1))
    allowed = jnp.concatenate(causal, axis=0)
    lane = lax.broadcasted_iota(jnp.int32, (rows, 128 - ROPE), 1)

    def stage(j):
        here = slice(j * rows, (j + 1) * rows)
        if j < blocks:
            source = 2 * (j % 4) + (core if j < 4 else 1 - core)
            out_of_range = jnp.logical_and(pos_ref[...] >= length - 4 * source, lane == 0)
            tails[here, ROPE:] = jnp.where(out_of_range, masked_value, 0.0).astype(bf16)
        else:
            tails[here, ROPE:] = jnp.zeros((rows, 128 - ROPE), bf16)
        tails[here, :ROPE] = latents[j][:, KVR:LAT]
        turned[:, here] = latents[j][:, :KVR].T

    def await_weights(pair):
        columns = slice(pair * 256, (pair + 1) * 256)
        for copy in ups[2 * pair:2 * pair + 2]:
            copy.wait()
        wv_turned[columns, :] = wv_ref[:, columns].T

    def project_up(pair, j):
        here = slice(j * rows, (j + 1) * rows)
        nope = latents[j][:, :KVR]
        columns = slice(pair * 256, (pair + 1) * 256)
        k = jnp.dot(nope, wk_ref[:, columns], preferred_element_type=f32).astype(bf16)
        v = jnp.dot(wv_turned[columns, :], turned[:, here], preferred_element_type=f32).astype(bf16)
        for i in range(2):
            slot = 2 * (pair % 2) + i
            keys[slot, here, :NOPE] = k[:, i * NOPE:(i + 1) * NOPE]
            keys[slot, here, NOPE:] = tails[here, :]
            values[2 * (pair % 3) + i, :, here] = v[i * VDIM:(i + 1) * VDIM]

    def score(h, j):
        here = slice(j * rows, (j + 1) * rows)
        s = jnp.dot(keys[h % 4, here], qt_ref[h], preferred_element_type=f32)
        if j >= blocks:
            s = jnp.where(allowed, s, masked_value)
        scores[h % 2, here] = s
        return jnp.max(s, axis=0, keepdims=True)

    def weigh(h, j, top):
        here = slice(j * rows, (j + 1) * rows)
        p = jnp.exp2((scores[h % 2, here] - top) * log2_scale)
        weights[h % 2, here] = p.astype(bf16)
        return jnp.sum(p, axis=0, keepdims=True)

    def gather_values(h, norm):
        acc = jnp.dot(values[2 * (h // 2 % 3) + h % 2], weights[h % 2], preferred_element_type=f32)
        out_ref[:, h * VDIM:(h + 1) * VDIM] = (acc / norm).T.astype(bf16)

    order = [blocks] + list(range(blocks))
    tops = []
    await_weights(0)
    for j in order:
        stage(j)
        project_up(0, j)
        tops.append(score(0, j))
    for h in range(heads):
        top = functools.reduce(jnp.maximum, tops)
        tops = []
        norms = []
        if h % 2 == 0 and h + 2 < heads:
            await_weights(h // 2 + 1)
        for i, j in enumerate(order):
            if h // 2 * 2 + 2 < heads and i % 2 == h % 2:
                project_up(h // 2 + 1, j)
            if h + 1 < heads:
                tops.append(score(h + 1, j))
            norms.append(weigh(h, j, top))
            if i == 2 and h > 0:
                gather_values(h - 1, norm)
        norm = functools.reduce(jnp.add, norms)
    gather_values(heads - 1, norm)


def attention(prefix_len, pos, qt, w_key_up, w_value_up, cached, turns, new_blocks):
    heads, _, tokens = qt.shape
    rows = pos.shape[0]
    blocks = 8
    total = rows * (blocks + 1)
    return pl.pallas_call(
        functools.partial(attention_kernel, turns),
        in_specs=[smem()] + [vmem()] * 2 + [hbm()] * 2 + [vmem()] * (2 + len(new_blocks)),
        out_specs=[vmem(), vmem()],
        out_shape=[
            jax.ShapeDtypeStruct((tokens, heads * VDIM), bf16),
            jax.ShapeDtypeStruct((8, 128), f32),
        ],
        scratch_shapes=[
            pltpu.VMEM((total, 128), bf16),
            pltpu.VMEM((4, total, QWIDE), bf16),
            pltpu.VMEM((6, VDIM, total), bf16),
            pltpu.VMEM((2, total, tokens), f32),
            pltpu.VMEM((2, total, tokens), bf16),
            pltpu.VMEM((rows, LAT), bf16),
            pltpu.VMEM((KVR, total), bf16),
            pltpu.VMEM(w_key_up.shape, bf16),
            pltpu.VMEM(w_value_up.shape, bf16),
            pltpu.VMEM(w_value_up.shape[::-1], bf16),
            pltpu.SemaphoreType.DMA((heads,)),
        ],
        compiler_params=pltpu.CompilerParams(vmem_limit_bytes=32 * MIB),
        cost_estimate=pl.CostEstimate(flops=4 * heads * tokens * total * 512, bytes_accessed=4 * MIB,
                                      transcendentals=heads * tokens * total),
        name="attention",
    )(prefix_len, pos, qt, w_key_up, w_value_up, *cached, *new_blocks)


def shards(
    hidden,
    w_kv_a,
    kv_gain,
    q_latent,
    w_q_b,
    w_key_up,
    w_value_up,
    pool,
    page_table,
    prefix_len,
    decode_owner,
):

    def tensor_permute(x, step):
        return lax.ppermute(x, "tensor", [(i, step(i)) for i in range(8)])

    up = lambda i: (i + 2) % 8
    down = lambda i: (i - 2) % 8
    far = lambda i: (i + 4) % 8
    other = lambda i: i ^ 1

    outgoing, pos = select(page_table, pool)
    outgoing = outgoing.reshape(page_table.shape[0], -1, LAT)
    incoming = lax.all_to_all(outgoing, "group", split_axis=0, concat_axis=0, tiled=True)
    own_block = incoming.reshape(pos.shape[0], LAT)

    frequency = jnp.asarray((rope_base ** (-2.0 * np.arange(HALF) / ROPE)).astype(np.float32)[:, None])

    qt, queried = make_queries(prefix_len, frequency, q_latent, w_q_b)

    partial_sum = project(hidden, w_kv_a.T)
    partner_sum = tensor_permute(partial_sum, other)
    own, to_up, to_down, to_far = combine(partial_sum, partner_sum)
    from_down = tensor_permute(to_up, up)
    from_up = tensor_permute(to_down, down)
    from_far = tensor_permute(to_far, far)
    latent, share = finish(prefix_len, frequency, own, from_down, from_up, from_far, kv_gain[None, :])
    latents = [latent, tensor_permute(latent, up), tensor_permute(latent, down), tensor_permute(latent, far)]

    def x_permute(turn):
        return lax.ppermute(share, "group", [(i, i // 4 * 4 + (i + turn) % 4) for i in range(32)])

    columns = [[4 * z + x for z in range(8)] for x in range(4)]
    addressed = address(decode_owner, [share, x_permute(1), x_permute(2), x_permute(3)])
    arrived = lax.all_to_all(addressed, "group", 0, 0, tiled=True, axis_index_groups=columns)

    same_core = lax.all_to_all(
        four_copies(own_block, latent, queried), "tensor", 0, 0, tiled=True, axis_index_groups=[[0, 2, 4, 6], [1, 3, 5, 7]]
    )
    same_core = again(same_core, addressed, *latents[1:])
    cached = [same_core, tensor_permute(same_core, other)]
    attn_out, attended = attention(prefix_len, pos, qt, w_key_up, w_value_up, cached, (0, 3, 1, 2), latents)
    decode_pages = pick(decode_owner, arrived, attended)
    return (attn_out, decode_pages)


def solution(mesh):
    return jax.shard_map(
        shards,
        mesh=mesh,
        in_specs=(
            P("group", "tensor"),
            P("tensor", None),
            P(),
            P("group", None),
            P(None, "tensor"),
            P(None, "tensor"),
            P(None, "tensor"),
            P("group", "tensor", None),
            P(),
            P(),
            P(),
        ),
        out_specs=(P("group", "tensor"), P(("group", "tensor"), None)),
        check_vma=False,
    )
```
